1024 devices in a mesh: row: 4 (over x), col: 256 (over y, z, core).
Axes of the slice: x: 4, y: 4, z: 32, core: 2. Of those that a mesh axis runs over, the one named last changes fastest.
Arguments:
- tokens: bfloat16 [256, 8192], P('col', 'row'), may hold values from -6 to 6
- out_grad: bfloat16 [256, 8192], P('col', 'row'), may hold values from -1.5 to 1.5
- gate_weight: bfloat16 [8192, 28672], P('row', 'col'), may hold values from -0.0625 to 0.0625
- up_weight: bfloat16 [8192, 28672], P('row', 'col'), may hold values from -0.0625 to 0.0625
- down_weight: bfloat16 [8192, 28672], P('row', 'col'), may hold values from -0.0625 to 0.0625
Outputs:
- in_grad: bfloat16 [256, 8192], P('col', 'row')
- gate_grad: bfloat16 [8192, 28672], P('row', 'col')
- up_grad: bfloat16 [8192, 28672], P('row', 'col')
- down_grad: bfloat16 [8192, 28672], P('row', 'col')
The draws below stay inside these ranges and needn't reach their ends.
All inputs are finite; a program needn't handle non-finite values.
Results may differ from the reference program's by a relative error of at most 0.005.
Values may be sent and summed in bfloat16 or wider, within the bound.
A program may use at most 32 MiB of HBM per device.

```python
import jax
import jax.numpy as jnp
from jax import lax

D = 8192
FF = 28672
TOKENS = 256


def block_levels(key, shape, shards, least, top_value):
    level, own = 1.0, jax.random.fold_in(key, 6)
    for dim, shards_of in shards:
        steps = jnp.exp(jax.random.uniform(jax.random.fold_in(own, dim), (shards_of,), jnp.float32, least / len(shards), top_value / len(shards)))
        level = level * jnp.repeat(steps, shape[dim] // shards_of).reshape([-1 if axis == dim else 1 for axis in range(len(shape))])
    return level


def scatter_about(rng, dims, width, bound, pieces=(), kind=jnp.bfloat16):
    entries = width * jax.random.normal(rng, dims, jnp.float32)
    if pieces:
        entries = entries * block_levels(rng, dims, pieces, -0.22, 0.18)
    return jnp.clip(entries, -bound, bound).astype(kind)


def setup_inputs(seed: int = 0) -> dict:
    splits = jax.random.split(jax.random.key(seed), 6)
    return {
        "tokens": scatter_about(splits[0], (TOKENS, D), 1.0, 6.0, ((0, 256), (1, 4))),
        "out_grad": scatter_about(splits[1], (TOKENS, D), 0.25, 1.5, ((0, 256), (1, 4))),
        "gate_weight": scatter_about(splits[2], (D, FF), D ** -0.5, 0.0625, ((0, 4), (1, 256))),
        "up_weight": scatter_about(splits[3], (D, FF), D ** -0.5, 0.0625, ((0, 4), (1, 256))),
        "down_weight": scatter_about(splits[4], (D, FF), D ** -0.5, 0.0625, ((0, 4), (1, 256))),
    }


def contract_rows(left, right):
    return lax.dot_general(left, right, (((0,), (0,)), ((), ())), preferred_element_type=jnp.float32)


def contract_cols(left, right):
    return lax.dot_general(left, right, (((1,), (1,)), ((), ())), preferred_element_type=jnp.float32)


def reference(tokens, out_grad, gate_weight, up_weight, down_weight):
    gate = jnp.dot(tokens, gate_weight, preferred_element_type=jnp.float32)
    up = jnp.dot(tokens, up_weight, preferred_element_type=jnp.float32)
    hidden_grad = jnp.dot(out_grad, down_weight, preferred_element_type=jnp.float32)
    sig = 1.0 / (1.0 + jnp.exp(-gate))
    silu = gate * sig
    hidden = (silu * up).astype(jnp.bfloat16)
    up_delta = (hidden_grad * silu).astype(jnp.bfloat16)
    gate_delta = (hidden_grad * up * sig * (1.0 + gate * (1.0 - sig))).astype(jnp.bfloat16)
    down_grad = contract_rows(out_grad, hidden).astype(jnp.bfloat16)
    gate_grad = contract_rows(tokens, gate_delta).astype(jnp.bfloat16)
    up_grad = contract_rows(tokens, up_delta).astype(jnp.bfloat16)
    in_grad = (contract_cols(gate_delta, gate_weight) + contract_cols(up_delta, up_weight)).astype(jnp.bfloat16)
    return in_grad, gate_grad, up_grad, down_grad
```

```python
import functools

import jax
import jax.numpy as jnp
from jax import lax
from jax.experimental import pallas as pl
from jax.experimental.pallas import tpu as pltpu
from jax.sharding import PartitionSpec as P

MESH = pl.DeviceIdType.MESH
F32, BF16 = jnp.float32, jnp.bfloat16
NY, NZ = 4, 32

KS = (0, 1, -1, 2, -2, 3, -3, 4)
SS = (0, -1, 1, 2)
CHUNKS = 4


def slot(k, core, dy, s):
    return ((KS.index(k) * 2 + core) * 4 + dy) * 4 + SS.index(s)


def spreads(k):
    out = [(s, k, s) for s in (-1, 1, 2)]
    if k == 3:
        out += [(3, 4, -1), (4, 4, 0)]
    if k == -3:
        out += [(-3, 4, 1), (-2, 4, 2)]
    return out


def near_far(k, s):
    dz = -(4 * k + s) % NZ
    dz = dz - NZ if dz > 16 else dz
    for low, high, f in ((-4, 3, 0), (4, 11, 8), (-12, -5, -8), (12, 16, 12), (-15, -13, -12)):
        if low <= dz <= high:
            return dz - f, f
    raise ValueError(dz)


FARS = (8, -8, 12, -12)
NEAR = {}
for _k in KS:
    for _s in SS:
        _r, _f = near_far(_k, _s)
        NEAR.setdefault(_r, []).append((_f, _k, _s))
RS = tuple(sorted(r for r in NEAR if r))
PARTNERS = (
    [(d, 0, 0, 0) for d in (1, 2, 3)]
    + [(0, d, 0, 0) for d in (1, 2, 3)]
    + [(0, 0, d, 0) for d in (-4, -3, -2, -1, 1, 2, 3, 4)]
    + [(0, 0, 0, 1)]
)


def kernel(
    tok_ref, grd_ref, gate_ref, up_ref, down_ref,
    in_ref, gate_out, up_out, down_out,
    own32, G, F, At, Ag, WT, part, XR, D, Pm, S1, R1, S2, R2, S3, R3, S4, R4, GW,
    zs, zr, ys, yr, cs, cr, xs, xrs, ds_, dr, s1s, s1r, s2s, s2r, s3s, s3r, s4s, s4r, wl, wo,
):
    x = lax.axis_index("row")
    col = lax.axis_index("col")
    core, z, y = col % 2, (col // 2) % NZ, col // (2 * NZ)

    def peer(dx, dy, dz, dc):
        return (
            (x + dx + 4) % 4,
            (((y + dy + NY) % NY) * NZ + (z + dz + NZ) % NZ) * 2 + (core + dc) % 2,
        )

    sends = []

    def copy(src, dst, ssem, rsem, to):
        return pltpu.make_async_remote_copy(
            src_ref=src, dst_ref=dst, send_sem=ssem, recv_sem=rsem, device_id=to, device_id_type=MESH
        )

    def send(src, dst, ssem, rsem, to):
        c = copy(src, dst, ssem, rsem, to)
        c.start()
        sends.append(c)

    def arrived(buf, sem):
        copy(buf, buf, sem, sem, peer(0, 0, 0, 1)).wait_recv()

    barrier = pltpu.get_barrier_semaphore()
    for p in PARTNERS:
        pl.semaphore_signal(barrier, inc=1, device_id=peer(*p), device_id_type=MESH)

    loads = [
        pltpu.make_async_copy(ref, WT.at[pl.ds(128 * i, 112)], wl.at[i])
        for i, ref in enumerate((gate_ref, up_ref, down_ref))
    ]
    for c in loads:
        c.start()
    for i in range(3):
        WT[128 * i + 112:128 * i + 128, :] = jnp.zeros((16, 2048), BF16)

    for i, ref in enumerate((tok_ref, grd_ref)):
        row = ref[...].astype(F32)
        for n in range(16):
            own32[16 * i + n:16 * i + n + 1, :] = row[:, 128 * n:128 * n + 128]
    G[0] = own32[...].astype(BF16)

    pl.semaphore_wait(barrier, len(PARTNERS))

    def zslot(k, s):
        return G.at[slot(k, 0, 0, s)]

    def zsem(k, s):
        return KS.index(k) * 4 + SS.index(s)

    def z_send(step, src, k, s):
        i = zsem(k, s)
        send(src, zslot(k, s), zs.at[i], zr.at[i], peer(0, 0, step, 0))

    def z_wait(k, s):
        arrived(zslot(k, s), zr.at[zsem(k, s)])

    def relay(k):
        if 0 <= k < 3:
            z_send(4, zslot(k, 0), k + 1, 0)
        if -3 < k <= 0:
            z_send(-4, zslot(k, 0), k - 1, 0)

    def spread(k):
        for step, k2, s in spreads(k):
            z_send(step, zslot(k, 0), k2, s)

    def y_send(k):
        for s in SS:
            if s != 0 or k == 4:
                z_wait(k, s)
        i = KS.index(k)
        for d in (1, 2, 3):
            send(
                G.at[pl.ds(slot(k, 0, 0, 0), 4)], G.at[pl.ds(slot(k, 0, d, 0), 4)],
                ys.at[i * 3 + d - 1], yr.at[i * 3 + d - 1], peer(0, d, 0, 0),
            )

    def c_send(k):
        i = KS.index(k)
        for d in (1, 2, 3):
            arrived(G.at[pl.ds(slot(k, 0, d, 0), 4)], yr.at[i * 3 + d - 1])
        send(
            G.at[pl.ds(slot(k, 0, 0, 0), 16)], G.at[pl.ds(slot(k, 1, 0, 0), 16)],
            cs.at[i], cr.at[i], peer(0, 0, 0, 1),
        )

    def rows_in_place(k):
        i = KS.index(k)
        arrived(G.at[pl.ds(slot(k, 1, 0, 0), 16)], cr.at[i])
        for c in (0, 1):
            first = slot(k, c, 0, 0)
            F[c] = G[first:first + 16].astype(F32).reshape(512, 128)
            for n in range(16):
                cols = slice(128 * n, 128 * n + 128)
                At[first:first + 16, cols] = F[c, pl.ds(n, 16, stride=32), :].astype(BF16)
                Ag[first:first + 16, cols] = F[c, pl.ds(16 + n, 16, stride=32), :].astype(BF16)

    def forward(i):
        rows = slice(64 * i, 64 * i + 64)
        nt = (((1,), (1,)), ((), ()))
        gu = lax.dot_general(At[rows, :], WT[0:256, :], nt, preferred_element_type=F32)
        hg = lax.dot_general(Ag[rows, :], WT[256:384, :], nt, preferred_element_type=F32)
        part[i, :, :, 0:256] = gu.reshape(4, 16, 256)
        part[i, :, :, 256:384] = hg.reshape(4, 16, 128)
        for d in (1, 2, 3):
            send(
                part.at[i, (x + d) % 4], XR.at[i, d - 1],
                xs.at[i * 3 + d - 1], xrs.at[i * 3 + d - 1], peer(d, 0, 0, 0),
            )

    def activate(i):
        for d in (1, 2, 3):
            arrived(XR.at[i, d - 1], xrs.at[i * 3 + d - 1])
        total = part[i, x] + XR[i, 0] + XR[i, 1] + XR[i, 2]
        gate, up, hidden_grad = total[:, 0:128], total[:, 128:256], total[:, 256:384]
        sig = 1.0 / (1.0 + jnp.exp(-gate))
        silu = gate * sig
        D[i, x, :, 0:128] = (hidden_grad * up * sig * (1.0 + gate * (1.0 - sig))).astype(BF16)
        D[i, x, :, 128:256] = (hidden_grad * silu).astype(BF16)
        D[i, x, :, 256:384] = (silu * up).astype(BF16)
        for d in (1, 2, 3):
            send(
                D.at[i, x], D.at[i, x],
                ds_.at[i * 3 + d - 1], dr.at[i * 3 + d - 1], peer(d, 0, 0, 0),
            )

    def back(i):
        for d in (1, 2, 3):
            arrived(D.at[i, (x - d + 4) % 4], dr.at[i * 3 + d - 1])
        delta = D[i, :, :, 0:256].reshape(64, 256)
        for n in range(8):
            out = jnp.dot(delta, WT[0:256, 256 * n:256 * n + 256], preferred_element_type=F32)
            for h in (0, 1):
                Pm[pl.ds(1024 * i + 2 * n + h, 64, stride=16), :] = out[:, 128 * h:128 * h + 128]
        for j in (2 * i, 2 * i + 1):
            S1[j] = Pm[512 * j + 256:512 * j + 512, :].astype(BF16)
            send(S1.at[j], R1.at[j], s1s.at[j], s1r.at[j], peer(0, 0, 0, 1))

    def over_y(i):
        for j in (0, 1):
            k = 2 * i + j
            arrived(R1.at[k], s1r.at[k])
            both = Pm[512 * k:512 * k + 256, :] + R1[k].astype(F32)
            Pm[512 * k:512 * k + 64, :] = both[0:64]
            for d in (1, 2, 3):
                S2[i, d - 1, 64 * j:64 * j + 64, :] = both[64 * d:64 * d + 64].astype(BF16)
        for d in (1, 2, 3):
            send(
                S2.at[i, d - 1], R2.at[i, d - 1],
                s2s.at[i * 3 + d - 1], s2r.at[i * 3 + d - 1], peer(0, -d, 0, 0),
            )

    def after_y(i):
        for d in (1, 2, 3):
            arrived(R2.at[i, d - 1], s2r.at[i * 3 + d - 1])
        for j in (0, 1):
            k = 2 * i + j
            total = Pm[512 * k:512 * k + 64, :]
            for d in (1, 2, 3):
                total = total + R2[i, d - 1, 64 * j:64 * j + 64, :].astype(F32)
            for n, s in enumerate(SS):
                piece = total[16 * n:16 * n + 16]
                r, f = near_far(KS[k], s)
                if r == 0:
                    Pm[512 * k + 16 * n:512 * k + 16 * n + 16, :] = piece
                else:
                    at = NEAR[r].index((f, KS[k], s))
                    S3[RS.index(r), 16 * at:16 * at + 16, :] = piece.astype(BF16)

    def held(k, s):
        at = 512 * KS.index(k) + 16 * SS.index(s)
        return Pm[at:at + 16, :]

    def at_relay(f):
        total = None
        for r, entries in NEAR.items():
            for n, (f2, k, s) in enumerate(entries):
                if f2 == f:
                    term = held(k, s) if r == 0 else R3[RS.index(r), 16 * n:16 * n + 16, :].astype(F32)
                    total = term if total is None else total + term
        return total

    relay(0)
    spread(0)
    for k in (1, -1):
        z_wait(k, 0)
        relay(k)
        spread(k)
    y_send(0)
    for k in (2, -2):
        z_wait(k, 0)
        relay(k)
        spread(k)
    for k in (1, -1):
        y_send(k)
    c_send(0)
    for k in (3, -3):
        z_wait(k, 0)
        spread(k)
    for k in (2, -2):
        y_send(k)
    for k in (1, -1):
        c_send(k)
    for c in loads:
        c.wait()
    for k in (0, 1):
        rows_in_place(k)
    forward(0)
    for k in (2, -2):
        c_send(k)
    for k in (3, -3, 4):
        y_send(k)
    for k in (-1, 2):
        rows_in_place(k)
    forward(1)
    activate(0)
    for k in (3, -3, 4):
        c_send(k)
    for k in (-2, 3):
        rows_in_place(k)
    forward(2)
    for k in (-3, 4):
        rows_in_place(k)
    forward(3)
    activate(1)
    back(0)
    activate(2)
    activate(3)
    back(1)
    over_y(0)
    back(2)
    over_y(1)
    over_y(2)
    back(3)
    over_y(3)
    for i in range(CHUNKS):
        after_y(i)
    for i, r in enumerate(RS):
        n = 16 * len(NEAR[r])
        send(S3.at[i, pl.ds(0, n)], R3.at[i, pl.ds(0, n)], s3s.at[i], s3r.at[i], peer(0, 0, r, 0))
    for i, r in enumerate(RS):
        arrived(R3.at[i, pl.ds(0, 16 * len(NEAR[r]))], s3r.at[i])
    for i, f in enumerate(FARS):
        S4[i] = at_relay(f)
        send(S4.at[i], R4.at[i], s4s.at[i], s4r.at[i], peer(0, 0, f, 0))

    tn = (((0,), (0,)), ((), ()))
    deltas = D[:, :, :, 0:256].reshape(256, 256)
    hidden = D[:, :, :, 256:384].reshape(256, 128)
    for n in range(8):
        cols = slice(256 * n, 256 * n + 256)
        GW[0:256, cols] = lax.dot_general(deltas, At[:, cols], tn, preferred_element_type=F32).astype(BF16)
        GW[256:384, cols] = lax.dot_general(hidden, Ag[:, cols], tn, preferred_element_type=F32).astype(BF16)
    stores = [
        pltpu.make_async_copy(GW.at[pl.ds(128 * i, 112)], ref, wo.at[i])
        for i, ref in enumerate((gate_out, up_out, down_out))
    ]
    for c in stores:
        c.start()
    mine = at_relay(0)
    for i in range(4):
        arrived(R4.at[i], s4r.at[i])
        mine = mine + R4[i]
    for n in range(16):
        in_ref[:, 128 * n:128 * n + 128] = mine[n:n + 1, :].astype(BF16)
    for c in sends:
        c.wait_send()
    for c in stores:
        c.wait()


def body(tokens, out_grad, gate_weight, up_weight, down_weight):
    vmem = pl.BlockSpec(memory_space=pltpu.VMEM)
    anywhere = pl.BlockSpec(memory_space=pl.ANY)
    wide = jax.ShapeDtypeStruct((112, 2048), BF16)
    dma = lambda n: pltpu.SemaphoreType.DMA((n,))
    in_grad, gate_grad, up_grad, down_grad = pl.pallas_call(
        kernel,
        name="swiglu_backward",
        out_shape=(jax.ShapeDtypeStruct((1, 2048), BF16), wide, wide, wide),
        in_specs=[vmem, vmem, anywhere, anywhere, anywhere],
        out_specs=(vmem, anywhere, anywhere, anywhere),
        scratch_shapes=[
            pltpu.VMEM((32, 128), F32),
            pltpu.VMEM((256, 32, 128), BF16),
            pltpu.VMEM((2, 512, 128), F32),
            pltpu.VMEM((256, 2048), BF16),
            pltpu.VMEM((256, 2048), BF16),
            pltpu.VMEM((384, 2048), BF16),
            pltpu.VMEM((4, 4, 16, 384), F32),
            pltpu.VMEM((4, 3, 16, 384), F32),
            pltpu.VMEM((4, 4, 16, 384), BF16),
            pltpu.VMEM((4096, 128), F32),
            pltpu.VMEM((8, 256, 128), BF16),
            pltpu.VMEM((8, 256, 128), BF16),
            pltpu.VMEM((4, 3, 128, 128), BF16),
            pltpu.VMEM((4, 3, 128, 128), BF16),
            pltpu.VMEM((len(RS), 64, 128), BF16),
            pltpu.VMEM((len(RS), 64, 128), BF16),
            pltpu.VMEM((4, 16, 128), F32),
            pltpu.VMEM((4, 16, 128), F32),
            pltpu.VMEM((384, 2048), BF16),
            dma(32), dma(32), dma(24), dma(24), dma(8), dma(8), dma(12), dma(12), dma(12), dma(12),
            dma(8), dma(8), dma(12), dma(12), dma(len(RS)), dma(len(RS)), dma(4), dma(4), dma(3), dma(3),
        ],
        compiler_params=pltpu.CompilerParams(
            collective_id=0, has_side_effects=True, vmem_limit_bytes=48 * 2 ** 20
        ),
    )(tokens, out_grad, gate_weight.T, up_weight.T, down_weight.T)
    return in_grad, gate_grad.T, up_grad.T, down_grad.T


def solution(mesh):
    placed = (P("col", "row"), P("col", "row"), P("row", "col"), P("row", "col"), P("row", "col"))
    return jax.shard_map(
        body,
        mesh=mesh,
        in_specs=placed,
        out_specs=(P("col", "row"), P("row", "col"), P("row", "col"), P("row", "col")),
        check_vma=False,
    )
```

```python
import functools

import jax
import jax.numpy as jnp
from jax import lax
from jax.experimental import pallas as pl
from jax.experimental.pallas import tpu as pltpu
from jax.sharding import PartitionSpec as P

MESH = pl.DeviceIdType.MESH
F32, BF16 = jnp.float32, jnp.bfloat16
NY, NZ = 4, 32

KS = (0, 1, -1, 2, -2, 3, -3, 4)
SS = (0, -1, 1, 2)
CHUNKS = 4


def slot(k, core, dy, s):
    return ((KS.index(k) * 2 + core) * 4 + dy) * 4 + SS.index(s)


def spreads(k):
    out = [(s, k, s) for s in (-1, 1, 2)]
    if k == 3:
        out += [(3, 4, -1), (4, 4, 0)]
    if k == -3:
        out += [(-3, 4, 1), (-2, 4, 2)]
    return out


def near_far(k, s):
    dz = -(4 * k + s) % NZ
    dz = dz - NZ if dz > 16 else dz
    for low, high, f in ((-4, 3, 0), (4, 11, 8), (-12, -5, -8), (12, 16, 12), (-15, -13, -12)):
        if low <= dz <= high:
            return dz - f, f
    raise ValueError(dz)


FARS = (8, -8, 12, -12)
NEAR = {}
for _k in KS:
    for _s in SS:
        _r, _f = near_far(_k, _s)
        NEAR.setdefault(_r, []).append((_f, _k, _s))
RS = tuple(sorted(r for r in NEAR if r))
PARTNERS = (
    [(d, 0, 0, 0) for d in (1, 2, 3)]
    + [(0, d, 0, 0) for d in (1, 2, 3)]
    + [(0, 0, d, 0) for d in (-4, -3, -2, -1, 1, 2, 3, 4)]
    + [(0, 0, 0, 1)]
)


def kernel(
    tok_ref, grd_ref, gate_ref, up_ref, down_ref,
    in_ref, gate_out, up_out, down_out,
    rows, own32, G, F, At, Ag, WT, part, XR, D, Pm, S1, R1, S2, R2, S3, R3, S4, R4, GW,
    zs, zr, ys, yr, cs, cr, xs, xrs, ds_, dr, s1s, s1r, s2s, s2r, s3s, s3r, s4s, s4r, wl, wo,
):
    x = lax.axis_index("row")
    col = lax.axis_index("col")
    core, z, y = col % 2, (col // 2) % NZ, col // (2 * NZ)

    def peer(dx, dy, dz, dc):
        return (
            (x + dx + 4) % 4,
            (((y + dy + NY) % NY) * NZ + (z + dz + NZ) % NZ) * 2 + (core + dc) % 2,
        )

    sends = []

    def copy(src, dst, ssem, rsem, to):
        return pltpu.make_async_remote_copy(
            src_ref=src, dst_ref=dst, send_sem=ssem, recv_sem=rsem, device_id=to, device_id_type=MESH
        )

    def send(src, dst, ssem, rsem, to):
        c = copy(src, dst, ssem, rsem, to)
        c.start()
        sends.append(c)

    def arrived(buf, sem):
        copy(buf, buf, sem, sem, peer(0, 0, 0, 1)).wait_recv()

    inputs = [
        pltpu.make_async_copy(ref, rows.at[i], wl.at[3 + i]) for i, ref in enumerate((tok_ref, grd_ref))
    ]
    for c in inputs:
        c.start()
    barrier = pltpu.get_barrier_semaphore()
    for p in PARTNERS:
        pl.semaphore_signal(barrier, inc=1, device_id=peer(*p), device_id_type=MESH)

    for i in range(3):
        WT[128 * i + 112:128 * i + 128, :] = jnp.zeros((16, 2048), BF16)

    for i in range(2):
        inputs[i].wait()
        row = rows[i].astype(F32)
        for n in range(16):
            own32[16 * i + n:16 * i + n + 1, :] = row[:, 128 * n:128 * n + 128]
    G[0] = own32[...].astype(BF16)

    pl.semaphore_wait(barrier, len(PARTNERS))

    def zslot(k, s):
        return G.at[slot(k, 0, 0, s)]

    def zsem(k, s):
        return KS.index(k) * 4 + SS.index(s)

    def z_send(step, src, k, s):
        i = zsem(k, s)
        send(src, zslot(k, s), zs.at[i], zr.at[i], peer(0, 0, step, 0))

    def z_wait(k, s):
        arrived(zslot(k, s), zr.at[zsem(k, s)])

    def relay(k):
        if 0 <= k < 3:
            z_send(4, zslot(k, 0), k + 1, 0)
        if -3 < k <= 0:
            z_send(-4, zslot(k, 0), k - 1, 0)

    def spread(k):
        for step, k2, s in spreads(k):
            z_send(step, zslot(k, 0), k2, s)

    def y_send(k):
        for s in SS:
            if s != 0 or k == 4:
                z_wait(k, s)
        i = KS.index(k)
        for d in (1, 2, 3):
            send(
                G.at[pl.ds(slot(k, 0, 0, 0), 4)], G.at[pl.ds(slot(k, 0, d, 0), 4)],
                ys.at[i * 3 + d - 1], yr.at[i * 3 + d - 1], peer(0, d, 0, 0),
            )

    def c_send(k):
        i = KS.index(k)
        for d in (1, 2, 3):
            arrived(G.at[pl.ds(slot(k, 0, d, 0), 4)], yr.at[i * 3 + d - 1])
        send(
            G.at[pl.ds(slot(k, 0, 0, 0), 16)], G.at[pl.ds(slot(k, 1, 0, 0), 16)],
            cs.at[i], cr.at[i], peer(0, 0, 0, 1),
        )

    def rows_in_place(k):
        i = KS.index(k)
        arrived(G.at[pl.ds(slot(k, 1, 0, 0), 16)], cr.at[i])
        for c in (0, 1):
            first = slot(k, c, 0, 0)
            F[c] = G[first:first + 16].astype(F32).reshape(512, 128)
            for n in range(16):
                cols = slice(128 * n, 128 * n + 128)
                At[first:first + 16, cols] = F[c, pl.ds(n, 16, stride=32), :].astype(BF16)
                Ag[first:first + 16, cols] = F[c, pl.ds(16 + n, 16, stride=32), :].astype(BF16)

    def forward(i):
        rws = slice(64 * i, 64 * i + 64)
        nt = (((1,), (1,)), ((), ()))
        gu = lax.dot_general(At[rws, :], WT[0:256, :], nt, preferred_element_type=F32)
        hg = lax.dot_general(Ag[rws, :], WT[256:384, :], nt, preferred_element_type=F32)
        part[i, :, :, 0:256] = gu.reshape(4, 16, 256)
        part[i, :, :, 256:384] = hg.reshape(4, 16, 128)
        for d in (1, 2, 3):
            send(
                part.at[i, (x + d) % 4], XR.at[i, d - 1],
                xs.at[i * 3 + d - 1], xrs.at[i * 3 + d - 1], peer(d, 0, 0, 0),
            )

    def activate(i):
        for d in (1, 2, 3):
            arrived(XR.at[i, d - 1], xrs.at[i * 3 + d - 1])
        total = part[i, x] + XR[i, 0] + XR[i, 1] + XR[i, 2]
        gate, up, hidden_grad = total[:, 0:128], total[:, 128:256], total[:, 256:384]
        sig = 1.0 / (1.0 + jnp.exp(-gate))
        silu = gate * sig
        D[i, x, :, 0:128] = (hidden_grad * up * sig * (1.0 + gate * (1.0 - sig))).astype(BF16)
        D[i, x, :, 128:256] = (hidden_grad * silu).astype(BF16)
        D[i, x, :, 256:384] = (silu * up).astype(BF16)
        for d in (1, 2, 3):
            send(
                D.at[i, x], D.at[i, x],
                ds_.at[i * 3 + d - 1], dr.at[i * 3 + d - 1], peer(d, 0, 0, 0),
            )

    def back(i):
        for d in (1, 2, 3):
            arrived(D.at[i, (x - d + 4) % 4], dr.at[i * 3 + d - 1])
        delta = D[i, :, :, 0:256].reshape(64, 256)
        for n in range(8):
            out = jnp.dot(delta, WT[0:256, 256 * n:256 * n + 256], preferred_element_type=F32)
            for h in (0, 1):
                Pm[pl.ds(1024 * i + 2 * n + h, 64, stride=16), :] = out[:, 128 * h:128 * h + 128]
        for j in (2 * i, 2 * i + 1):
            S1[j] = Pm[512 * j + 256:512 * j + 512, :].astype(BF16)
            send(S1.at[j], R1.at[j], s1s.at[j], s1r.at[j], peer(0, 0, 0, 1))

    def over_y(i):
        for j in (0, 1):
            k = 2 * i + j
            arrived(R1.at[k], s1r.at[k])
            both = Pm[512 * k:512 * k + 256, :] + R1[k].astype(F32)
            Pm[512 * k:512 * k + 64, :] = both[0:64]
            for d in (1, 2, 3):
                S2[i, d - 1, 64 * j:64 * j + 64, :] = both[64 * d:64 * d + 64].astype(BF16)
        for d in (1, 2, 3):
            send(
                S2.at[i, d - 1], R2.at[i, d - 1],
                s2s.at[i * 3 + d - 1], s2r.at[i * 3 + d - 1], peer(0, -d, 0, 0),
            )

    def after_y(i):
        for d in (1, 2, 3):
            arrived(R2.at[i, d - 1], s2r.at[i * 3 + d - 1])
        for j in (0, 1):
            k = 2 * i + j
            total = Pm[512 * k:512 * k + 64, :]
            for d in (1, 2, 3):
                total = total + R2[i, d - 1, 64 * j:64 * j + 64, :].astype(F32)
            for n, s in enumerate(SS):
                piece = total[16 * n:16 * n + 16]
                r, f = near_far(KS[k], s)
                if r == 0:
                    Pm[512 * k + 16 * n:512 * k + 16 * n + 16, :] = piece
                else:
                    at = NEAR[r].index((f, KS[k], s))
                    S3[RS.index(r), 16 * at:16 * at + 16, :] = piece.astype(BF16)

    def held(k, s):
        at = 512 * KS.index(k) + 16 * SS.index(s)
        return Pm[at:at + 16, :]

    def at_relay(f):
        total = None
        for r, entries in NEAR.items():
            for n, (f2, k, s) in enumerate(entries):
                if f2 == f:
                    term = held(k, s) if r == 0 else R3[RS.index(r), 16 * n:16 * n + 16, :].astype(F32)
                    total = term if total is None else total + term
        return total

    relay(0)
    spread(0)
    loads = [
        pltpu.make_async_copy(ref, WT.at[pl.ds(128 * i, 112)], wl.at[i])
        for i, ref in enumerate((gate_ref, up_ref, down_ref))
    ]
    for c in loads:
        c.start()
    for k in (1, -1):
        z_wait(k, 0)
        relay(k)
        spread(k)
    y_send(0)
    for k in (2, -2):
        z_wait(k, 0)
        relay(k)
        spread(k)
    for k in (1, -1):
        y_send(k)
    c_send(0)
    for k in (3, -3):
        z_wait(k, 0)
        spread(k)
    for k in (2, -2):
        y_send(k)
    for k in (1, -1):
        c_send(k)
    for c in loads:
        c.wait()
    for k in (0, 1):
        rows_in_place(k)
    forward(0)
    for k in (2, -2):
        c_send(k)
    for k in (3, -3, 4):
        y_send(k)
    for k in (-1, 2):
        rows_in_place(k)
    forward(1)
    activate(0)
    for k in (3, -3, 4):
        c_send(k)
    for k in (-2, 3):
        rows_in_place(k)
    forward(2)
    for k in (-3, 4):
        rows_in_place(k)
    forward(3)
    activate(1)
    back(0)
    activate(2)
    activate(3)
    back(1)
    over_y(0)
    back(2)
    over_y(1)
    over_y(2)
    back(3)
    over_y(3)
    for i in range(CHUNKS):
        after_y(i)
    for i, r in enumerate(RS):
        n = 16 * len(NEAR[r])
        send(S3.at[i, pl.ds(0, n)], R3.at[i, pl.ds(0, n)], s3s.at[i], s3r.at[i], peer(0, 0, r, 0))
    for i, r in enumerate(RS):
        arrived(R3.at[i, pl.ds(0, 16 * len(NEAR[r]))], s3r.at[i])
    for i, f in enumerate(FARS):
        S4[i] = at_relay(f)
        send(S4.at[i], R4.at[i], s4s.at[i], s4r.at[i], peer(0, 0, f, 0))

    tn = (((0,), (0,)), ((), ()))
    deltas = D[:, :, :, 0:256].reshape(256, 256)
    hidden = D[:, :, :, 256:384].reshape(256, 128)
    for n in range(8):
        cols = slice(256 * n, 256 * n + 256)
        GW[0:256, cols] = lax.dot_general(deltas, At[:, cols], tn, preferred_element_type=F32).astype(BF16)
        GW[256:384, cols] = lax.dot_general(hidden, Ag[:, cols], tn, preferred_element_type=F32).astype(BF16)
    stores = [
        pltpu.make_async_copy(GW.at[pl.ds(128 * i, 112)], ref, wo.at[i])
        for i, ref in enumerate((gate_out, up_out, down_out))
    ]
    for c in stores:
        c.start()
    mine = at_relay(0)
    for i in range(4):
        arrived(R4.at[i], s4r.at[i])
        mine = mine + R4[i]
    for n in range(16):
        in_ref[:, 128 * n:128 * n + 128] = mine[n:n + 1, :].astype(BF16)
    for c in sends:
        c.wait_send()
    for c in stores:
        c.wait()


def hand_over(*refs):
    copies = [pltpu.make_async_copy(refs[i], refs[4 + i], refs[8].at[i]) for i in range(4)]
    for c in copies:
        c.start()
    for c in copies:
        c.wait()


def body(tokens, out_grad, gate_weight, up_weight, down_weight):
    vmem = pl.BlockSpec(memory_space=pltpu.VMEM)
    anywhere = pl.BlockSpec(memory_space=pl.ANY)
    wide = jax.ShapeDtypeStruct((112, 2048), BF16)
    shapes = (jax.ShapeDtypeStruct((1, 2048), BF16), wide, wide, wide)
    dma = lambda n: pltpu.SemaphoreType.DMA((n,))
    operands = (tokens, out_grad, gate_weight.T, up_weight.T, down_weight.T)
    pinned = [pltpu.with_memory_space_constraint(v, pltpu.HBM) for v in operands]
    results = pl.pallas_call(
        kernel,
        name="swiglu_backward",
        out_shape=shapes,
        in_specs=[anywhere] * 5,
        out_specs=(vmem, anywhere, anywhere, anywhere),
        scratch_shapes=[
            pltpu.VMEM((2, 1, 2048), BF16),
            pltpu.VMEM((32, 128), F32),
            pltpu.VMEM((256, 32, 128), BF16),
            pltpu.VMEM((2, 512, 128), F32),
            pltpu.VMEM((256, 2048), BF16),
            pltpu.VMEM((256, 2048), BF16),
            pltpu.VMEM((384, 2048), BF16),
            pltpu.VMEM((4, 4, 16, 384), F32),
            pltpu.VMEM((4, 3, 16, 384), F32),
            pltpu.VMEM((4, 4, 16, 384), BF16),
            pltpu.VMEM((4096, 128), F32),
            pltpu.VMEM((8, 256, 128), BF16),
            pltpu.VMEM((8, 256, 128), BF16),
            pltpu.VMEM((4, 3, 128, 128), BF16),
            pltpu.VMEM((4, 3, 128, 128), BF16),
            pltpu.VMEM((len(RS), 64, 128), BF16),
            pltpu.VMEM((len(RS), 64, 128), BF16),
            pltpu.VMEM((4, 16, 128), F32),
            pltpu.VMEM((4, 16, 128), F32),
            pltpu.VMEM((384, 2048), BF16),
            dma(32), dma(32), dma(24), dma(24), dma(8), dma(8), dma(12), dma(12), dma(12), dma(12),
            dma(8), dma(8), dma(12), dma(12), dma(len(RS)), dma(len(RS)), dma(4), dma(4), dma(5), dma(3),
        ],
        compiler_params=pltpu.CompilerParams(
            collective_id=0, has_side_effects=True, vmem_limit_bytes=48 * 2 ** 20
        ),
    )(*pinned)
    in_grad, gate_grad, up_grad, down_grad = pl.pallas_call(
        hand_over,
        name="hand_over",
        out_shape=shapes,
        in_specs=[anywhere] * 4,
        out_specs=(anywhere,) * 4,
        scratch_shapes=[dma(4)],
    )(*[pltpu.with_memory_space_constraint(v, pltpu.VMEM) for v in results])
    return in_grad, gate_grad.T, up_grad.T, down_grad.T


def solution(mesh):
    placed = (P("col", "row"), P("col", "row"), P("row", "col"), P("row", "col"), P("row", "col"))
    return jax.shard_map(
        body,
        mesh=mesh,
        in_specs=placed,
        out_specs=(P("col", "row"), P("row", "col"), P("row", "col"), P("row", "col")),
        check_vma=False,
    )
```

```python
import functools

import jax
import jax.numpy as jnp
from jax import lax
from jax.experimental import pallas as pl
from jax.experimental.pallas import tpu as pltpu
from jax.sharding import PartitionSpec as P

MESH = pl.DeviceIdType.MESH
F32, BF16 = jnp.float32, jnp.bfloat16
NY, NZ = 4, 32

KS = (0, 1, -1, 2, -2, 3, -3, 4)
SS = (0, -1, 1, 2)
CHUNKS = 4


def slot(k, core, dy, s):
    return ((KS.index(k) * 2 + core) * 4 + dy) * 4 + SS.index(s)


def spreads(k):
    out = [(s, k, s) for s in (-1, 1, 2)]
    if k == 3:
        out += [(3, 4, -1), (4, 4, 0)]
    if k == -3:
        out += [(-3, 4, 1), (-2, 4, 2)]
    return out


def near_far(k, s):
    dz = -(4 * k + s) % NZ
    dz = dz - NZ if dz > 16 else dz
    for low, high, f in ((-4, 3, 0), (4, 11, 8), (-12, -5, -8), (12, 16, 12), (-15, -13, -12)):
        if low <= dz <= high:
            return dz - f, f
    raise ValueError(dz)


FARS = (8, -8, 12, -12)
NEAR = {}
for _k in KS:
    for _s in SS:
        _r, _f = near_far(_k, _s)
        NEAR.setdefault(_r, []).append((_f, _k, _s))
RS = tuple(sorted(r for r in NEAR if r))
PARTNERS = (
    [(d, 0, 0, 0) for d in (1, 2, 3)]
    + [(0, d, 0, 0) for d in (1, 2, 3)]
    + [(0, 0, d, 0) for d in (-4, -3, -2, -1, 1, 2, 3, 4)]
    + [(0, 0, 0, 1)]
)


def kernel(
    tok_ref, grd_ref, gate_ref, up_ref, down_ref,
    in_ref, gate_out, up_out, down_out,
    rows, own32, G, F, At, Ag, WT, part, XR, D, Pm, S1, R1, S2, R2, S3, R3, S4, R4, GW,
    zs, zr, ys, yr, cs, cr, xs, xrs, ds_, dr, s1s, s1r, s2s, s2r, s3s, s3r, s4s, s4r, wl, wo,
):
    x = lax.axis_index("row")
    col = lax.axis_index("col")
    core, z, y = col % 2, (col // 2) % NZ, col // (2 * NZ)

    def peer(dx, dy, dz, dc):
        return (
            (x + dx + 4) % 4,
            (((y + dy + NY) % NY) * NZ + (z + dz + NZ) % NZ) * 2 + (core + dc) % 2,
        )

    sends = []

    def copy(src, dst, ssem, rsem, to):
        return pltpu.make_async_remote_copy(
            src_ref=src, dst_ref=dst, send_sem=ssem, recv_sem=rsem, device_id=to, device_id_type=MESH
        )

    def send(src, dst, ssem, rsem, to):
        c = copy(src, dst, ssem, rsem, to)
        c.start()
        sends.append(c)

    def arrived(buf, sem):
        copy(buf, buf, sem, sem, peer(0, 0, 0, 1)).wait_recv()

    inputs = [
        pltpu.make_async_copy(ref, rows.at[i], wl.at[3 + i]) for i, ref in enumerate((tok_ref, grd_ref))
    ]
    for c in inputs:
        c.start()
    barrier = pltpu.get_barrier_semaphore()
    for p in PARTNERS:
        pl.semaphore_signal(barrier, inc=1, device_id=peer(*p), device_id_type=MESH)

    for i in range(3):
        WT[128 * i + 112:128 * i + 128, :] = jnp.zeros((16, 2048), BF16)

    for i in range(2):
        inputs[i].wait()
        row = rows[i].astype(F32)
        for n in range(16):
            own32[16 * i + n:16 * i + n + 1, :] = row[:, 128 * n:128 * n + 128]
    G[0] = own32[...].astype(BF16)

    pl.semaphore_wait(barrier, len(PARTNERS))

    def zslot(k, s):
        return G.at[slot(k, 0, 0, s)]

    def zsem(k, s):
        return KS.index(k) * 4 + SS.index(s)

    def z_send(step, src, k, s):
        i = zsem(k, s)
        send(src, zslot(k, s), zs.at[i], zr.at[i], peer(0, 0, step, 0))

    def z_wait(k, s):
        arrived(zslot(k, s), zr.at[zsem(k, s)])

    def relay(k):
        if 0 <= k < 3:
            z_send(4, zslot(k, 0), k + 1, 0)
        if -3 < k <= 0:
            z_send(-4, zslot(k, 0), k - 1, 0)

    def spread(k):
        for step, k2, s in spreads(k):
            z_send(step, zslot(k, 0), k2, s)

    def y_send(k):
        for s in SS:
            if s != 0 or k == 4:
                z_wait(k, s)
        i = KS.index(k)
        for d in (1, 2, 3):
            send(
                G.at[pl.ds(slot(k, 0, 0, 0), 4)], G.at[pl.ds(slot(k, 0, d, 0), 4)],
                ys.at[i * 3 + d - 1], yr.at[i * 3 + d - 1], peer(0, d, 0, 0),
            )

    def c_send(k):
        i = KS.index(k)
        for d in (1, 2, 3):
            arrived(G.at[pl.ds(slot(k, 0, d, 0), 4)], yr.at[i * 3 + d - 1])
        send(
            G.at[pl.ds(slot(k, 0, 0, 0), 16)], G.at[pl.ds(slot(k, 1, 0, 0), 16)],
            cs.at[i], cr.at[i], peer(0, 0, 0, 1),
        )

    def rows_in_place(k):
        i = KS.index(k)
        arrived(G.at[pl.ds(slot(k, 1, 0, 0), 16)], cr.at[i])
        for c in (0, 1):
            first = slot(k, c, 0, 0)
            F[c] = G[first:first + 16].astype(F32).reshape(512, 128)
            for n in range(16):
                cols = slice(128 * n, 128 * n + 128)
                At[first:first + 16, cols] = F[c, pl.ds(n, 16, stride=32), :].astype(BF16)
                Ag[first:first + 16, cols] = F[c, pl.ds(16 + n, 16, stride=32), :].astype(BF16)

    def forward(i):
        rws = slice(64 * i, 64 * i + 64)
        nt = (((1,), (1,)), ((), ()))
        gu = lax.dot_general(At[rws, :], WT[0:256, :], nt, preferred_element_type=F32)
        hg = lax.dot_general(Ag[rws, :], WT[256:384, :], nt, preferred_element_type=F32)
        part[i, :, :, 0:256] = gu.reshape(4, 16, 256)
        part[i, :, :, 256:384] = hg.reshape(4, 16, 128)
        for d in (1, 2, 3):
            send(
                part.at[i, (x + d) % 4], XR.at[i, d - 1],
                xs.at[i * 3 + d - 1], xrs.at[i * 3 + d - 1], peer(d, 0, 0, 0),
            )

    def activate(i):
        for d in (1, 2, 3):
            arrived(XR.at[i, d - 1], xrs.at[i * 3 + d - 1])
        total = part[i, x] + XR[i, 0] + XR[i, 1] + XR[i, 2]
        gate, up, hidden_grad = total[:, 0:128], total[:, 128:256], total[:, 256:384]
        sig = 1.0 / (1.0 + jnp.exp(-gate))
        silu = gate * sig
        D[i, x, :, 0:128] = (hidden_grad * up * sig * (1.0 + gate * (1.0 - sig))).astype(BF16)
        D[i, x, :, 128:256] = (hidden_grad * silu).astype(BF16)
        D[i, x, :, 256:384] = (silu * up).astype(BF16)
        for d in (1, 2, 3):
            send(
                D.at[i, x], D.at[i, x],
                ds_.at[i * 3 + d - 1], dr.at[i * 3 + d - 1], peer(d, 0, 0, 0),
            )

    def back(i):
        for d in (1, 2, 3):
            arrived(D.at[i, (x - d + 4) % 4], dr.at[i * 3 + d - 1])
        delta = D[i, :, :, 0:256].reshape(64, 256)
        for n in range(8):
            out = jnp.dot(delta, WT[0:256, 256 * n:256 * n + 256], preferred_element_type=F32)
            for h in (0, 1):
                Pm[pl.ds(1024 * i + 2 * n + h, 64, stride=16), :] = out[:, 128 * h:128 * h + 128]
        for j in (2 * i, 2 * i + 1):
            S1[j] = Pm[512 * j + 256:512 * j + 512, :].astype(BF16)
            send(S1.at[j], R1.at[j], s1s.at[j], s1r.at[j], peer(0, 0, 0, 1))

    def over_y(i):
        for j in (0, 1):
            k = 2 * i + j
            arrived(R1.at[k], s1r.at[k])
            both = Pm[512 * k:512 * k + 256, :] + R1[k].astype(F32)
            Pm[512 * k:512 * k + 64, :] = both[0:64]
            for d in (1, 2, 3):
                S2[i, d - 1, 64 * j:64 * j + 64, :] = both[64 * d:64 * d + 64].astype(BF16)
        for d in (1, 2, 3):
            send(
                S2.at[i, d - 1], R2.at[i, d - 1],
                s2s.at[i * 3 + d - 1], s2r.at[i * 3 + d - 1], peer(0, -d, 0, 0),
            )

    def after_y(i):
        for d in (1, 2, 3):
            arrived(R2.at[i, d - 1], s2r.at[i * 3 + d - 1])
        for j in (0, 1):
            k = 2 * i + j
            total = Pm[512 * k:512 * k + 64, :]
            for d in (1, 2, 3):
                total = total + R2[i, d - 1, 64 * j:64 * j + 64, :].astype(F32)
            for n, s in enumerate(SS):
                piece = total[16 * n:16 * n + 16]
                r, f = near_far(KS[k], s)
                if r == 0:
                    Pm[512 * k + 16 * n:512 * k + 16 * n + 16, :] = piece
                else:
                    at = NEAR[r].index((f, KS[k], s))
                    S3[RS.index(r), 16 * at:16 * at + 16, :] = piece.astype(BF16)

    def held(k, s):
        at = 512 * KS.index(k) + 16 * SS.index(s)
        return Pm[at:at + 16, :]

    def at_relay(f):
        total = None
        for r, entries in NEAR.items():
            for n, (f2, k, s) in enumerate(entries):
                if f2 == f:
                    term = held(k, s) if r == 0 else R3[RS.index(r), 16 * n:16 * n + 16, :].astype(F32)
                    total = term if total is None else total + term
        return total

    relay(0)
    spread(0)
    loads = [
        pltpu.make_async_copy(ref, WT.at[pl.ds(128 * i, 112)], wl.at[i])
        for i, ref in enumerate((gate_ref, up_ref, down_ref))
    ]
    for c in loads:
        c.start()
    for k in (1, -1):
        z_wait(k, 0)
        relay(k)
        spread(k)
    y_send(0)
    for k in (2, -2):
        z_wait(k, 0)
        relay(k)
        spread(k)
    for k in (1, -1):
        y_send(k)
    c_send(0)
    for k in (2, -2):
        y_send(k)
    for k in (3, -3):
        z_wait(k, 0)
        spread(k)
    for k in (1, -1):
        c_send(k)
    for c in loads:
        c.wait()
    for k in (0, 1):
        rows_in_place(k)
    forward(0)
    for k in (3, -3, 4):
        y_send(k)
    for k in (2, -2):
        c_send(k)
    for k in (-1, 2):
        rows_in_place(k)
    forward(1)
    activate(0)
    for k in (3, -3, 4):
        c_send(k)
    for k in (-2, 3):
        rows_in_place(k)
    forward(2)
    for k in (-3, 4):
        rows_in_place(k)
    forward(3)
    activate(1)
    back(0)
    activate(2)
    activate(3)
    back(1)
    over_y(0)
    back(2)
    over_y(1)
    over_y(2)
    back(3)
    over_y(3)
    for i in range(CHUNKS):
        after_y(i)
    for i, r in enumerate(RS):
        n = 16 * len(NEAR[r])
        send(S3.at[i, pl.ds(0, n)], R3.at[i, pl.ds(0, n)], s3s.at[i], s3r.at[i], peer(0, 0, r, 0))
    for i, r in enumerate(RS):
        arrived(R3.at[i, pl.ds(0, 16 * len(NEAR[r]))], s3r.at[i])
    for i, f in enumerate(FARS):
        S4[i] = at_relay(f)
        send(S4.at[i], R4.at[i], s4s.at[i], s4r.at[i], peer(0, 0, f, 0))

    tn = (((0,), (0,)), ((), ()))
    deltas = D[:, :, :, 0:256].reshape(256, 256)
    hidden = D[:, :, :, 256:384].reshape(256, 128)
    for n in range(8):
        cols = slice(256 * n, 256 * n + 256)
        GW[0:256, cols] = lax.dot_general(deltas, At[:, cols], tn, preferred_element_type=F32).astype(BF16)
        GW[256:384, cols] = lax.dot_general(hidden, Ag[:, cols], tn, preferred_element_type=F32).astype(BF16)
    stores = [
        pltpu.make_async_copy(GW.at[pl.ds(128 * i, 112)], ref, wo.at[i])
        for i, ref in enumerate((gate_out, up_out, down_out))
    ]
    for c in stores:
        c.start()
    mine = at_relay(0)
    for i in range(4):
        arrived(R4.at[i], s4r.at[i])
        mine = mine + R4[i]
    for n in range(16):
        in_ref[:, 128 * n:128 * n + 128] = mine[n:n + 1, :].astype(BF16)
    for c in sends:
        c.wait_send()
    for c in stores:
        c.wait()


def hand_over(*refs):
    copies = [pltpu.make_async_copy(refs[i], refs[4 + i], refs[8].at[i]) for i in range(4)]
    for c in copies:
        c.start()
    for c in copies:
        c.wait()


def body(tokens, out_grad, gate_weight, up_weight, down_weight):
    vmem = pl.BlockSpec(memory_space=pltpu.VMEM)
    anywhere = pl.BlockSpec(memory_space=pl.ANY)
    wide = jax.ShapeDtypeStruct((112, 2048), BF16)
    shapes = (jax.ShapeDtypeStruct((1, 2048), BF16), wide, wide, wide)
    dma = lambda n: pltpu.SemaphoreType.DMA((n,))
    operands = (tokens, out_grad, gate_weight.T, up_weight.T, down_weight.T)
    pinned = [pltpu.with_memory_space_constraint(v, pltpu.HBM) for v in operands]
    results = pl.pallas_call(
        kernel,
        name="swiglu_backward",
        out_shape=shapes,
        in_specs=[anywhere] * 5,
        out_specs=(vmem, anywhere, anywhere, anywhere),
        scratch_shapes=[
            pltpu.VMEM((2, 1, 2048), BF16),
            pltpu.VMEM((32, 128), F32),
            pltpu.VMEM((256, 32, 128), BF16),
            pltpu.VMEM((2, 512, 128), F32),
            pltpu.VMEM((256, 2048), BF16),
            pltpu.VMEM((256, 2048), BF16),
            pltpu.VMEM((384, 2048), BF16),
            pltpu.VMEM((4, 4, 16, 384), F32),
            pltpu.VMEM((4, 3, 16, 384), F32),
            pltpu.VMEM((4, 4, 16, 384), BF16),
            pltpu.VMEM((4096, 128), F32),
            pltpu.VMEM((8, 256, 128), BF16),
            pltpu.VMEM((8, 256, 128), BF16),
            pltpu.VMEM((4, 3, 128, 128), BF16),
            pltpu.VMEM((4, 3, 128, 128), BF16),
            pltpu.VMEM((len(RS), 64, 128), BF16),
            pltpu.VMEM((len(RS), 64, 128), BF16),
            pltpu.VMEM((4, 16, 128), F32),
            pltpu.VMEM((4, 16, 128), F32),
            pltpu.VMEM((384, 2048), BF16),
            dma(32), dma(32), dma(24), dma(24), dma(8), dma(8), dma(12), dma(12), dma(12), dma(12),
            dma(8), dma(8), dma(12), dma(12), dma(len(RS)), dma(len(RS)), dma(4), dma(4), dma(5), dma(3),
        ],
        compiler_params=pltpu.CompilerParams(
            collective_id=0, has_side_effects=True, vmem_limit_bytes=48 * 2 ** 20
        ),
    )(*pinned)
    in_grad, gate_grad, up_grad, down_grad = pl.pallas_call(
        hand_over,
        name="hand_over",
        out_shape=shapes,
        in_specs=[anywhere] * 4,
        out_specs=(anywhere,) * 4,
        scratch_shapes=[dma(4)],
    )(*[pltpu.with_memory_space_constraint(v, pltpu.VMEM) for v in results])
    return in_grad, gate_grad.T, up_grad.T, down_grad.T


def solution(mesh):
    placed = (P("col", "row"), P("col", "row"), P("row", "col"), P("row", "col"), P("row", "col"))
    return jax.shard_map(
        body,
        mesh=mesh,
        in_specs=placed,
        out_specs=(P("col", "row"), P("row", "col"), P("row", "col"), P("row", "col")),
        check_vma=False,
    )
```
